512 devices in a mesh: dp: 32 (over x, z_lo, core), mp: 16 (over y, z_hi).
Axes of the slice: x: 4, y: 4, z: 16 (z_hi: 4, z_lo: 4; z = z_hi * 4 + z_lo), core: 2. Of those that a mesh axis runs over, the one named last changes fastest.
Arguments:
- reference_hidden_states: bfloat16 [512, 32, 8, 3072], P('dp', 'mp'), may hold values from -700 to 700
- policy_hidden_states: bfloat16 [512, 32, 8, 3072], P(('dp', 'mp')), may hold values from -700 to 700
- reference_norm_gain: float32 [3072], replicated, may hold values from 0.5 to 1.5
- policy_norm_gain: float32 [3072], replicated, may hold values from 0.5 to 1.5
- action_head_weight: bfloat16 [3072, 2048], P('mp'), may hold values from -0.3125 to 0.3125
- adapter_down_weight: bfloat16 [3072, 64], P('mp'), may hold values from -0.109375 to 0.109375
- adapter_up_weight: bfloat16 [2048, 64], P('mp'), may hold values from -0.75 to 0.75
- actions: int32 [512, 32, 8], P(('dp', 'mp')), may hold values from 0 to 2047
- agent_present_mask: int32 [512, 32, 8], P(('dp', 'mp')), may hold values 0 or 1
- behaviour_log_prob: float32 [512, 32, 8], P(('dp', 'mp')), may hold values from -16 to -9
- advantages: float32 [512, 32, 8], P(('dp', 'mp')), may hold values from -4 to 4
Outputs:
- grad_down: float32 [3072, 64], P('mp')
- grad_up: float32 [2048, 64], P('mp')
The draws below stay inside these ranges and needn't reach their ends.
All inputs are finite; a program needn't handle non-finite values. No bound on the sum of `agent_present_mask` on one device may be relied on, other than what follows from the above.
Results may differ from the reference program's by a relative error of at most 0.008.
Values may be sent and summed in bfloat16 or wider, within the bound.
No kernel may reach another device: no remote copies, remote signals or barrier semaphores. Data moves between devices by JAX's collectives and lax.ppermute only.
A program may use at most 64 MiB of HBM per device.

```python
import jax
import jax.numpy as jnp
from jax import lax

MODEL_WIDTH = 3072
ACTION_TOKENS = 2048
ADAPTER_RANK = 64
SLOTS = 32
STEPS = 8
SCENES = 512


def scaled_field(key, row_range):
    keys = jax.random.split(key, 3)
    array_shape = (SCENES, SLOTS, STEPS, MODEL_WIDTH)
    row_scale = jnp.exp(jax.random.uniform(keys[0], (SCENES, SLOTS, STEPS, 1), jnp.float32) * jnp.log(row_range))
    col_scale = jnp.exp(jax.random.uniform(keys[1], (MODEL_WIDTH,), jnp.float32) * jnp.log(10.0))
    base = jax.random.truncated_normal(keys[2], -4.0, 4.0, array_shape, jnp.float32)
    return base * row_scale * col_scale


def draw_reference_hidden_states(key, part):
    key = jax.random.fold_in(key, 11)
    return scaled_field(key, 10.0).astype(jnp.bfloat16)


def draw_policy_hidden_states(key, part):
    key = jax.random.fold_in(key, 23)
    return scaled_field(key, 10.0).astype(jnp.bfloat16)


def place_ends(result, key, smallest, top_value):
    place = [jax.random.randint(jax.random.fold_in(key, axis), (), 0, length) for axis, length in enumerate(result.shape)]
    widest = result.shape.index(max(result.shape))
    neighbour = place[:widest] + [(place[widest] + 1) % result.shape[widest]] + place[widest + 1:]
    return result.at[tuple(place)].set(smallest).at[tuple(neighbour)].set(top_value)


def level_of(stream_key, shape, cuts, least, top_value):
    loudness, own = 1.0, jax.random.fold_in(stream_key, 6)
    for axis_at, blocks in cuts:
        steps = jnp.exp(jax.random.uniform(jax.random.fold_in(own, axis_at), (blocks,), jnp.float32, least / len(cuts), top_value / len(cuts)))
        loudness = loudness * jnp.repeat(steps, shape[axis_at] // blocks).reshape([-1 if axis == axis_at else 1 for axis in range(len(shape))])
    return loudness


def centred(key, extent, scale, bound, shards=(), kind=jnp.bfloat16):
    entries = jax.random.normal(key, extent, jnp.float32) * scale
    if len(shards) > 0:
        entries = level_of(key, extent, shards, -0.22, 0.18) * entries
    return jnp.clip(entries, min=-bound, max=bound).astype(kind)


def setup_inputs(seed: int = 0) -> dict:
    key_list = jax.random.split(jax.random.key(seed), 12)
    return {
        "reference_hidden_states": draw_reference_hidden_states(jax.random.fold_in(key_list[11], 71), 0),
        "policy_hidden_states": draw_policy_hidden_states(jax.random.fold_in(key_list[11], 71), 0),
        "reference_norm_gain": jnp.clip(1.0 + 0.1 * jax.random.normal(key_list[2], (MODEL_WIDTH,), jnp.float32), 0.5, 1.5),
        "policy_norm_gain": jnp.clip(1.0 + 0.1 * jax.random.normal(key_list[3], (MODEL_WIDTH,), jnp.float32), 0.5, 1.5),
        "action_head_weight": centred(key_list[4], (MODEL_WIDTH, ACTION_TOKENS), (MODEL_WIDTH // 9) ** -0.5, 0.3125, ((0, 16),)),
        "adapter_down_weight": centred(key_list[5], (MODEL_WIDTH, ADAPTER_RANK), MODEL_WIDTH ** -0.5, 0.109375, ((0, 16),)),
        "adapter_up_weight": centred(key_list[6], (ACTION_TOKENS, ADAPTER_RANK), ADAPTER_RANK ** -0.5, 0.75, ((0, 16),)),
        "actions": place_ends(jax.random.randint(key_list[7], (SCENES, SLOTS, STEPS), 0, ACTION_TOKENS), jax.random.fold_in(key_list[7], 1), 0, ACTION_TOKENS - 1).astype(jnp.int32),
        "agent_present_mask": place_ends((jax.random.randint(key_list[8], (SCENES, SLOTS, STEPS), 0, 4) < 3).astype(jnp.int32), jax.random.fold_in(key_list[8], 1), 0, 1),
        "behaviour_log_prob": jnp.clip(-16.0 + 7.0 * jax.random.uniform(key_list[9], (SCENES, SLOTS, STEPS), jnp.float32) ** level_of(key_list[9], (SCENES, SLOTS, STEPS), ((0, 512),), -0.2, 0.2), -16.0, -9.0),
        "advantages": centred(key_list[10], (SCENES, SLOTS, STEPS), 1.0, 4.0, ((0, 512),), jnp.float32),
    }


NORM_EPS = 1e-05
CLIP_LOG = 2.0
KL_COEF = 0.25

def normalize(hidden, gain):
    values = hidden.astype(jnp.float32)
    mean_square = lax.optimization_barrier(jnp.mean(values * values, axis=-1, keepdims=True))
    return (values * lax.rsqrt(mean_square + NORM_EPS) * gain.astype(jnp.float32)).astype(jnp.bfloat16)

def log_probs(policy_logits):
    return policy_logits - jnp.log(lax.optimization_barrier(jnp.sum(jnp.exp(policy_logits), axis=-1, keepdims=True)))

def rows_loss(policy_logits, ref_logp, chosen_ids, mask_rows, old_rows, adv_rows):
    logp = log_probs(policy_logits)
    picked = lax.broadcasted_iota(jnp.int32, policy_logits.shape, 1) == chosen_ids[:, None]
    chosen = lax.optimization_barrier(jnp.sum(jnp.where(picked, logp, 0.0), axis=-1))
    surrogate = adv_rows * jnp.exp(CLIP_LOG * jnp.tanh((chosen - old_rows) / CLIP_LOG))
    divergence = lax.optimization_barrier(jnp.sum(jnp.exp(logp) * (logp - ref_logp.astype(policy_logits.dtype)), axis=-1))
    return jnp.sum(mask_rows.astype(policy_logits.dtype) * (KL_COEF * divergence - surrogate))

def reference(reference_hidden_states, policy_hidden_states, reference_norm_gain, policy_norm_gain, action_head_weight, adapter_down_weight, adapter_up_weight, actions, agent_present_mask, behaviour_log_prob, advantages):
    width = reference_hidden_states.shape[-1]

    def per_scene(sums, items):
        ref_rows, pol_rows, chosen_ids, mask_rows, old_rows, adv_rows = items
        ref_normed = normalize(ref_rows, reference_norm_gain).reshape(-1, width)
        policy_normed_hidden = normalize(pol_rows, policy_norm_gain).reshape(-1, width)
        ref_logp = log_probs(jnp.dot(ref_normed, action_head_weight, preferred_element_type=jnp.float32)).astype(jnp.bfloat16)
        adapter_product = jnp.dot(policy_normed_hidden, adapter_down_weight, preferred_element_type=jnp.float32).astype(jnp.bfloat16)
        policy_logits = jnp.dot(policy_normed_hidden, action_head_weight, preferred_element_type=jnp.float32) + lax.dot_general(adapter_product, adapter_up_weight, (((1,), (1,)), ((), ())), preferred_element_type=jnp.float32)
        logit_slopes = jax.grad(rows_loss)(policy_logits, ref_logp, chosen_ids.reshape(-1), mask_rows.reshape(-1), old_rows.reshape(-1), adv_rows.reshape(-1)).astype(jnp.bfloat16)
        up_grad = lax.dot_general(logit_slopes, adapter_product, (((0,), (0,)), ((), ())), preferred_element_type=jnp.float32)
        adapter_slopes = jnp.dot(logit_slopes, adapter_up_weight, preferred_element_type=jnp.float32).astype(jnp.bfloat16)
        down_grad = lax.dot_general(policy_normed_hidden, adapter_slopes, (((0,), (0,)), ((), ())), preferred_element_type=jnp.float32)
        return ((sums[0] + down_grad, sums[1] + up_grad), None)
    initial_values = (jnp.zeros(adapter_down_weight.shape, jnp.float32), jnp.zeros(adapter_up_weight.shape, jnp.float32))
    totals, unused = lax.scan(per_scene, initial_values, (reference_hidden_states, policy_hidden_states, actions, agent_present_mask, behaviour_log_prob, advantages))
    return (totals[0], totals[1])
```

```python
import functools

import jax
import jax.numpy as jnp
import numpy as np
from jax import lax
from jax.experimental import pallas as pl
from jax.experimental.pallas import tpu as pltpu
from jax.sharding import Mesh, PartitionSpec as P

NORM_EPS = 1e-05
CLIP_LOG = 2.0
KL_COEF = 0.25

X, ZL, C, Y, ZH = 4, 4, 2, 4, 4
WIDTH = 3072
TOKENS = 2048
RANK = 64
ROWS = 256
KY = WIDTH // Y
KM = KY // ZH
TM = TOKENS // (Y * ZH)
NB = TOKENS // (C * X)
PIECE = KY + ZH * 16
SHIFTS = (0, 1, 3, 2)
LANES = 384

bf16 = jnp.bfloat16
f32 = jnp.float32


def pairs(step):
    sizes = (X, C, Y)
    found = []
    for index in np.ndindex(*sizes):
        to = tuple(t % s for t, s in zip(step(*index), sizes))
        found.append(
            (int(np.ravel_multi_index(index, sizes)), int(np.ravel_multi_index(to, sizes)))
        )
    return found


def shift_first(v, k):
    return lax.ppermute(v, ("x", "c", "y"), pairs(lambda x, c, y: (x + k * (c == 0), c, y + k * (c == 1))))


def shift_second(v, k):
    return lax.ppermute(v, ("x", "c", "y"), pairs(lambda x, c, y: (x + k * (c == 1), c, y + k * (c == 0))))


def swap_cores(v):
    return lax.ppermute(v, "c", [(0, 1), (1, 0)])


def bdot(a, b, dims):
    return lax.dot_general(a, b, (dims, ((), ())), preferred_element_type=f32)


def kernel(
    place, pol_hbm, ref_hbm, pol_gain, ref_gain, rows8,
    p0, p1, p2, p3, p4, p5, p6, p7,
    keep, give,
    held, normed, acc, up, down, slopes, low_t, grad, hid, sems,
):
    x, y, c = place[0], place[1], place[2]
    parts = (p0, p1, p2, p3, p4, p5, p6, p7)
    first = [
        pltpu.make_async_copy(pol_hbm, hid.at[0], sems.at[8]),
        pltpu.make_async_copy(ref_hbm, hid.at[1], sems.at[9]),
    ]
    copies = [pltpu.make_async_copy(parts[i], held.at[i], sems.at[i]) for i in range(8)]
    for copy in first + copies:
        copy.start()

    acc[...] = jnp.zeros_like(acc)
    step = 32
    for which, gain in ((0, pol_gain), (1, ref_gain)):
        first[which].wait()

        def norm(i, carry, which=which, gain=gain):
            at = pl.ds(pl.multiple_of(i * step, step), step)
            v = hid[which, at, :].astype(f32)
            ms = jnp.sum(v * v, axis=-1, keepdims=True) * (1.0 / WIDTH)
            n = (v * lax.rsqrt(ms + NORM_EPS) * gain[...]).astype(bf16)
            for k in range(Y):
                normed[which, k, at, :] = n[:, k * KY : (k + 1) * KY]
            return carry

        lax.fori_loop(0, ROWS // step, norm, 0)

    for i in range(8):
        copies[i].wait()
        core = c if i < 4 else 1 - c
        k2 = SHIFTS[i % 4]

        def block(q, carry, i=i, core=core, k2=k2):
            k1 = jnp.where(q == 2, 3, jnp.where(q == 3, 2, q))
            kx = jnp.where(core == 0, k1, k2)
            ky = jnp.where(core == 0, k2, k1)
            xq = lax.rem(x + X - kx, X)
            ys = lax.rem(y + Y - ky, Y)
            j = core * X + xq
            w = held[i, q, 0:KY, :]
            for which in range(2):
                acc[which, j] += bdot(normed[which, ys], w, ((1,), (0,)))
            at = pl.ds(pl.multiple_of(xq * 16, 16), 16)
            e = held[i, q, KY:PIECE, :]

            @pl.when(core == 0)
            def _():
                for z in range(ZH):
                    up[ys, at, z * TM : (z + 1) * TM] = e[z * 16 : (z + 1) * 16, 0:TM]

            @pl.when(core == 1)
            def _():
                down[ys, at, :] = jnp.concatenate(
                    [e[z * 16 : (z + 1) * 16, 0:KM] for z in range(ZH)], axis=1
                )

            return carry

        lax.fori_loop(0, 4, block, 0)

    low = jnp.zeros((ROWS, RANK), f32)
    for k in range(Y):
        low += bdot(normed[0, k], down[k], ((1,), (1,)))
    low16 = low.astype(bf16)
    low_t[...] = low.T.astype(bf16)

    cols = rows8[...].T
    acts = cols[:, 0:1].astype(jnp.int32)
    mask, old, adv = cols[:, 1:2], cols[:, 2:3], cols[:, 3:4]
    iota = lax.broadcasted_iota(jnp.int32, (ROWS, NB), 1)

    def up_part(j):
        return up[j // 2, :, (j % 2) * NB : (j % 2 + 1) * NB]

    s_pol = jnp.zeros((ROWS, 1), f32)
    s_ref = jnp.zeros((ROWS, 1), f32)
    hit = jnp.zeros((ROWS, 1), f32)
    for j in range(8):
        v = acc[0, j] + bdot(low16, up_part(j), ((1,), (0,)))
        acc[0, j] = v
        s_pol += jnp.sum(jnp.exp(v), axis=-1, keepdims=True)
        hit += jnp.sum(jnp.where(iota == acts - j * NB, v, 0.0), axis=-1, keepdims=True)
        s_ref += jnp.sum(jnp.exp(acc[1, j]), axis=-1, keepdims=True)
    lse_pol, lse_ref = jnp.log(s_pol), jnp.log(s_ref)
    taken = hit - lse_pol
    t = jnp.tanh((taken - old) / CLIP_LOG)
    pull = mask * (adv * jnp.exp(CLIP_LOG * t) * (1.0 - t * t))
    div = jnp.zeros((ROWS, 1), f32)
    for j in range(8):
        logp = acc[0, j] - lse_pol
        gap = logp - (acc[1, j] - lse_ref).astype(bf16).astype(f32)
        p = jnp.exp(logp)
        div += jnp.sum(p * gap, axis=-1, keepdims=True)
        acc[0, j] = p
        acc[1, j] = gap
    scale = mask * KL_COEF
    base = pull - scale * div
    low_slopes = jnp.zeros((ROWS, RANK), f32)
    for j in range(8):
        s = acc[0, j] * (scale * acc[1, j] + base) - jnp.where(iota == acts - j * NB, pull, 0.0)
        s16 = s.astype(bf16)
        grad[:, j * NB : (j + 1) * NB] = bdot(low_t[...], s16, ((1,), (0,)))
        low_slopes += bdot(s16, up_part(j), ((1,), (1,)))
    low_slopes_t = low_slopes.T.astype(bf16)
    for k in range(Y):
        grad[:, TOKENS + k * KY : TOKENS + (k + 1) * KY] = bdot(low_slopes_t, normed[0, k], ((1,), (0,)))

    blank = jnp.zeros((8, LANES - TM - KM), f32)
    for out, core in ((keep, c), (give, 1 - c)):
        for xx in range(X):
            at = pl.ds(pl.multiple_of((xx * C + core) * 8, 8), 8)
            for m in range(Y * ZH):
                out[xx, m] = jnp.concatenate(
                    [
                        grad[at, m * TM : (m + 1) * TM],
                        grad[at, TOKENS + m * KM : TOKENS + (m + 1) * KM],
                        blank,
                    ],
                    axis=1,
                )


def local(ref_hidden, pol_hidden, ref_gain, pol_gain, head, down_w, up_w, actions, present, old, adv):
    x, y, c = lax.axis_index("x"), lax.axis_index("y"), lax.axis_index("c")
    piece = lax.dynamic_slice(head, (0, (c * X + x) * NB), (KM, NB))
    up_t = jnp.pad(up_w.T, ((0, 0), (0, NB - TM)))
    down_t = jnp.pad(down_w.T, ((0, 0), (0, NB - KM)))
    extra = lax.dynamic_slice(jnp.where(c == 0, up_t, down_t), (x * 16, 0), (16, NB))
    piece = jnp.concatenate([piece, extra], axis=0)
    along_z = lax.all_to_all(
        jnp.broadcast_to(piece[None], (ZH, KM + 16, NB)), "zh", 0, 0, tiled=True
    )
    mine = jnp.concatenate(
        [along_z[:, :KM].reshape(KY, NB), along_z[:, KM:].reshape(ZH * 16, NB)], axis=0
    )
    four = jnp.stack([mine] + [shift_first(mine, k) for k in SHIFTS[1:]])
    own = [four] + [shift_second(four, k) for k in SHIFTS[1:]]
    other = [swap_cores(v) for v in own]

    ref_rows = lax.all_to_all(
        ref_hidden.reshape(Y * ZH, ROWS // (Y * ZH), WIDTH), ("y", "zh"), 0, 0, tiled=True
    ).reshape(ROWS, WIDTH)
    pol_rows = pol_hidden.reshape(ROWS, WIDTH)
    rows8 = jnp.stack(
        [v.reshape(ROWS).astype(f32) for v in (actions, present, old, adv)]
        + [jnp.zeros((ROWS,), f32)] * 4
    )
    place = jnp.stack([x, y, c]).astype(jnp.int32)

    vmem = pl.BlockSpec(memory_space=pltpu.VMEM)
    hbm = pl.BlockSpec(memory_space=pl.ANY)
    out = jax.ShapeDtypeStruct((X, Y * ZH, 8, LANES), f32)
    keep, give = pl.pallas_call(
        kernel,
        out_shape=(out, out),
        in_specs=[pl.BlockSpec(memory_space=pltpu.SMEM), hbm, hbm, vmem, vmem, vmem] + [hbm] * 8,
        out_specs=(vmem, vmem),
        scratch_shapes=[
            pltpu.VMEM((8, 4, PIECE, NB), bf16),
            pltpu.VMEM((2, Y, ROWS, KY), bf16),
            pltpu.VMEM((2, C * X, ROWS, NB), f32),
            pltpu.VMEM((Y, RANK, TOKENS // Y), bf16),
            pltpu.VMEM((Y, RANK, KY), bf16),
            pltpu.VMEM((8, 128), bf16),
            pltpu.VMEM((RANK, ROWS), bf16),
            pltpu.VMEM((RANK, TOKENS + WIDTH), f32),
            pltpu.VMEM((2, ROWS, WIDTH), bf16),
            pltpu.SemaphoreType.DMA((10,)),
        ],
        compiler_params=pltpu.CompilerParams(vmem_limit_bytes=36 * 1024 * 1024),
        cost_estimate=pl.CostEstimate(
            flops=4 * ROWS * WIDTH * TOKENS, bytes_accessed=18 << 20, transcendentals=3 * ROWS * TOKENS
        ),
    )(
        place, pol_rows, ref_rows,
        pol_gain.reshape(1, WIDTH), ref_gain.reshape(1, WIDTH), rows8, *own, *other,
    )

    part = keep + swap_cores(give)
    part = lax.all_to_all(part.reshape(X * Y, ZH, 8, LANES), ("x", "y"), 0, 0, tiled=True).sum(0)
    part = jnp.broadcast_to(part[None], (ZL, ZH, 8, LANES)).reshape(ZL * ZH, 8, LANES)
    part = lax.all_to_all(part, ("zl", "zh"), 0, 0, tiled=True).sum(0)
    whole = lax.all_to_all(
        jnp.broadcast_to(part[None], (X * C, 8, LANES)), ("x", "c"), 0, 0, tiled=True
    ).reshape(RANK, LANES)
    return whole[:, TM : TM + KM].T, whole[:, :TM].T


def solution(mesh):
    wide = Mesh(mesh.devices.reshape(X, ZL, C, Y, ZH), ("x", "zl", "c", "y", "zh"))
    dp, mp = ("x", "zl", "c"), ("y", "zh")
    placed = (
        P(dp, mp, None, None),
        P(dp + mp, None, None, None),
        P(),
        P(),
        P(mp, None),
        P(mp, None),
        P(mp, None),
        P(dp + mp, None, None),
        P(dp + mp, None, None),
        P(dp + mp, None, None),
        P(dp + mp, None, None),
    )
    return jax.shard_map(
        local, mesh=wide, in_specs=placed, out_specs=(P(mp, None), P(mp, None)), check_vma=False
    )
```

```python
import functools

import jax
import jax.numpy as jnp
import numpy as np
from jax import lax
from jax.experimental import pallas as pl
from jax.experimental.pallas import tpu as pltpu
from jax.sharding import Mesh, PartitionSpec as P

NORM_EPS = 1e-05
CLIP_LOG = 2.0
KL_COEF = 0.25

X, ZL, C, Y, ZH = 4, 4, 2, 4, 4
WIDTH = 3072
TOKENS = 2048
RANK = 64
ROWS = 256
KY = WIDTH // Y
KM = KY // ZH
TM = TOKENS // (Y * ZH)
NB = TOKENS // (C * X)
PIECE = KY + ZH * 16
SHIFTS = (0, 1, 3, 2)
LANES = 384

bf16 = jnp.bfloat16
f32 = jnp.float32


def pairs(step):
    sizes = (X, C, Y)
    found = []
    for index in np.ndindex(*sizes):
        to = tuple(t % s for t, s in zip(step(*index), sizes))
        found.append(
            (int(np.ravel_multi_index(index, sizes)), int(np.ravel_multi_index(to, sizes)))
        )
    return found


def shift_first(v, k):
    return lax.ppermute(v, ("x", "c", "y"), pairs(lambda x, c, y: (x + k * (c == 0), c, y + k * (c == 1))))


def shift_second(v, k):
    return lax.ppermute(v, ("x", "c", "y"), pairs(lambda x, c, y: (x + k * (c == 1), c, y + k * (c == 0))))


def swap_cores(v):
    return lax.ppermute(v, "c", [(0, 1), (1, 0)])


def bdot(a, b, dims):
    return lax.dot_general(a, b, (dims, ((), ())), preferred_element_type=f32)


def kernel(
    place, pol_hbm, ref_hbm, pol_gain, ref_gain, rows8,
    p0, p1, p2, p3, p4, p5, p6, p7,
    keep, give,
    held, normed, acc, up, down, low_t, grad, hid, sems,
):
    x, y, c = place[0], place[1], place[2]
    parts = (p0, p1, p2, p3, p4, p5, p6, p7)
    first = [
        pltpu.make_async_copy(pol_hbm, hid.at[0], sems.at[8]),
        pltpu.make_async_copy(ref_hbm, hid.at[1], sems.at[9]),
    ]
    copies = [pltpu.make_async_copy(parts[i], held.at[i], sems.at[i]) for i in range(8)]
    for copy in first + copies:
        copy.start()

    step = 32
    for which, gain in ((0, pol_gain), (1, ref_gain)):
        first[which].wait()

        def norm(i, carry, which=which, gain=gain):
            at = pl.ds(pl.multiple_of(i * step, step), step)
            v = hid[which, at, :].astype(f32)
            ms = jnp.sum(v * v, axis=-1, keepdims=True) * (1.0 / WIDTH)
            n = (v * lax.rsqrt(ms + NORM_EPS) * gain[...]).astype(bf16)
            for k in range(Y):
                normed[k, pl.ds(pl.multiple_of(which * ROWS + i * step, step), step), :] = n[:, k * KY : (k + 1) * KY]
            return carry

        lax.fori_loop(0, ROWS // step, norm, 0)


    def order(q):
        return jnp.where(q == 2, 3, jnp.where(q == 3, 2, q))

    for half in range(2):
        core = c if half == 0 else 1 - c
        for i in range(4):
            copies[half * 4 + i].wait()

        def column(s, carry, half=half, core=core):
            xq = lax.rem(x + X - order(s), X)
            j = core * X + xq
            at = pl.ds(pl.multiple_of(xq * 16, 16), 16)
            ysn, blk = [], []
            for n in range(4):
                ysn.append(lax.rem(y + Y - SHIFTS[n], Y))
                blk.append((half * 4 + jnp.where(core == 0, n, s), jnp.where(core == 0, s, n)))
            total = None
            for n in range(4):
                part = bdot(normed[ysn[n]], held[blk[n][0], blk[n][1], 0:KY, :], ((1,), (0,)))
                total = part if total is None else total + part
            acc[j] = total

            for n in range(4):
                ys = ysn[n]
                e = held[blk[n][0], blk[n][1], KY:PIECE, :]

                @pl.when(core == 0)
                def _(ys=ys, e=e):
                    for z in range(ZH):
                        up[ys, at, z * TM : (z + 1) * TM] = e[z * 16 : (z + 1) * 16, 0:TM]

                @pl.when(core == 1)
                def _(ys=ys, e=e):
                    down[ys, at, :] = jnp.concatenate(
                        [e[z * 16 : (z + 1) * 16, 0:KM] for z in range(ZH)], axis=1
                    )

            return carry

        lax.fori_loop(0, 4, column, 0)

    low = jnp.zeros((ROWS, RANK), f32)
    for k in range(Y):
        low += bdot(normed[k, 0:ROWS], down[k], ((1,), (1,)))
    low16 = low.astype(bf16)
    low_t[...] = low.T.astype(bf16)

    cols = rows8[...].T
    acts = cols[:, 0:1].astype(jnp.int32)
    mask, old, adv = cols[:, 1:2], cols[:, 2:3], cols[:, 3:4]
    iota = lax.broadcasted_iota(jnp.int32, (ROWS, NB), 1)

    def up_part(j):
        return up[j // 2, :, (j % 2) * NB : (j % 2 + 1) * NB]

    s_pol = jnp.zeros((ROWS, 1), f32)
    s_ref = jnp.zeros((ROWS, 1), f32)
    hit = jnp.zeros((ROWS, 1), f32)
    for j in range(8):
        v = acc[j, 0:ROWS] + bdot(low16, up_part(j), ((1,), (0,)))
        acc[j, 0:ROWS] = v
        s_pol += jnp.sum(jnp.exp(v), axis=-1, keepdims=True)
        hit += jnp.sum(jnp.where(iota == acts - j * NB, v, 0.0), axis=-1, keepdims=True)
        s_ref += jnp.sum(jnp.exp(acc[j, ROWS:]), axis=-1, keepdims=True)
    lse_pol, lse_ref = jnp.log(s_pol), jnp.log(s_ref)
    taken = hit - lse_pol
    t = jnp.tanh((taken - old) / CLIP_LOG)
    pull = mask * (adv * jnp.exp(CLIP_LOG * t) * (1.0 - t * t))
    div = jnp.zeros((ROWS, 1), f32)
    for j in range(8):
        logp = acc[j, 0:ROWS] - lse_pol
        gap = logp - (acc[j, ROWS:] - lse_ref).astype(bf16).astype(f32)
        p = jnp.exp(logp)
        div += jnp.sum(p * gap, axis=-1, keepdims=True)
        acc[j, 0:ROWS] = p
        acc[j, ROWS:] = gap
    scale = mask * KL_COEF
    base = pull - scale * div
    low_slopes = jnp.zeros((ROWS, RANK), f32)
    for j in range(8):
        s = acc[j, 0:ROWS] * (scale * acc[j, ROWS:] + base) - jnp.where(iota == acts - j * NB, pull, 0.0)
        s16 = s.astype(bf16)
        grad[:, j * NB : (j + 1) * NB] = bdot(low_t[...], s16, ((1,), (0,)))
        low_slopes += bdot(s16, up_part(j), ((1,), (1,)))
    low_slopes_t = low_slopes.T.astype(bf16)
    for k in range(Y):
        grad[:, TOKENS + k * KY : TOKENS + (k + 1) * KY] = bdot(low_slopes_t, normed[k, 0:ROWS], ((1,), (0,)))

    blank = jnp.zeros((8, LANES - TM - KM), f32)
    for out, core in ((keep, c), (give, 1 - c)):
        for xx in range(X):
            at = pl.ds(pl.multiple_of((xx * C + core) * 8, 8), 8)
            for m in range(Y * ZH):
                sums = jnp.concatenate(
                    [
                        grad[at, m * TM : (m + 1) * TM],
                        grad[at, TOKENS + m * KM : TOKENS + (m + 1) * KM],
                        blank,
                    ],
                    axis=1,
                )
                out[xx, m] = sums.astype(out.dtype)


def local(ref_hidden, pol_hidden, ref_gain, pol_gain, head, down_w, up_w, actions, present, old, adv):
    x, y, c = lax.axis_index("x"), lax.axis_index("y"), lax.axis_index("c")
    piece = lax.dynamic_slice(head, (0, (c * X + x) * NB), (KM, NB))
    up_t = jnp.pad(up_w.T, ((0, 0), (0, NB - TM)))
    down_t = jnp.pad(down_w.T, ((0, 0), (0, NB - KM)))
    extra = lax.dynamic_slice(jnp.where(c == 0, up_t, down_t), (x * 16, 0), (16, NB))
    piece = jnp.concatenate([piece, extra], axis=0)
    along_z = lax.all_to_all(
        jnp.broadcast_to(piece[None], (ZH, KM + 16, NB)), "zh", 0, 0, tiled=True
    )
    mine = jnp.concatenate(
        [along_z[:, :KM].reshape(KY, NB), along_z[:, KM:].reshape(ZH * 16, NB)], axis=0
    )
    four = jnp.stack([mine] + [shift_first(mine, k) for k in SHIFTS[1:]])
    own = [four] + [shift_second(four, k) for k in SHIFTS[1:]]
    other = [swap_cores(v) for v in own]

    ref_hidden, guard = lax.optimization_barrier((ref_hidden, swap_cores(mine[:16, :NB])))
    ref_rows = lax.all_to_all(
        ref_hidden.reshape(Y * ZH, ROWS // (Y * ZH), WIDTH), ("y", "zh"), 0, 0, tiled=True
    ).reshape(ROWS, WIDTH)
    pol_rows = pol_hidden.reshape(ROWS, WIDTH)
    rows8 = jnp.stack(
        [v.reshape(ROWS).astype(f32) for v in (actions, present, old, adv)]
        + [jnp.zeros((ROWS,), f32)] * 3
        + [guard[0].astype(f32)]
    )
    place = jnp.stack([x, y, c]).astype(jnp.int32)

    vmem = pl.BlockSpec(memory_space=pltpu.VMEM)
    hbm = pl.BlockSpec(memory_space=pl.ANY)
    out = jax.ShapeDtypeStruct((X, Y * ZH, 8, LANES), f32)
    keep, give = pl.pallas_call(
        kernel,
        out_shape=(out, jax.ShapeDtypeStruct(out.shape, bf16)),
        in_specs=[pl.BlockSpec(memory_space=pltpu.SMEM), hbm, hbm, vmem, vmem, vmem] + [hbm] * 8,
        out_specs=(vmem, vmem),
        scratch_shapes=[
            pltpu.VMEM((8, 4, PIECE, NB), bf16),
            pltpu.VMEM((Y, 2 * ROWS, KY), bf16),
            pltpu.VMEM((C * X, 2 * ROWS, NB), f32),
            pltpu.VMEM((Y, RANK, TOKENS // Y), bf16),
            pltpu.VMEM((Y, RANK, KY), bf16),
            pltpu.VMEM((RANK, ROWS), bf16),
            pltpu.VMEM((RANK, TOKENS + WIDTH), f32),
            pltpu.VMEM((2, ROWS, WIDTH), bf16),
            pltpu.SemaphoreType.DMA((10,)),
        ],
        compiler_params=pltpu.CompilerParams(vmem_limit_bytes=36 * 1024 * 1024),
        cost_estimate=pl.CostEstimate(
            flops=4 * ROWS * WIDTH * TOKENS, bytes_accessed=18 << 20, transcendentals=3 * ROWS * TOKENS
        ),
    )(
        place, pol_rows, ref_rows,
        pol_gain.reshape(1, WIDTH), ref_gain.reshape(1, WIDTH), rows8, *own, *other,
    )

    part = (keep + swap_cores(give).astype(f32)).astype(bf16)
    part = lax.all_to_all(part.reshape(X * Y, ZH, 8, LANES), ("x", "y"), 0, 0, tiled=True)
    part = part.astype(f32).sum(0).astype(bf16)
    part = jnp.broadcast_to(part[None], (ZL, ZH, 8, LANES)).reshape(ZL * ZH, 8, LANES)
    part = lax.all_to_all(part, ("zl", "zh"), 0, 0, tiled=True).astype(f32).sum(0)
    whole = lax.all_to_all(
        jnp.broadcast_to(part[None], (X * C, 8, LANES)), ("x", "c"), 0, 0, tiled=True
    ).reshape(RANK, LANES)
    return whole[:, TM : TM + KM].T, whole[:, :TM].T


def solution(mesh):
    wide = Mesh(mesh.devices.reshape(X, ZL, C, Y, ZH), ("x", "zl", "c", "y", "zh"))
    dp, mp = ("x", "zl", "c"), ("y", "zh")
    placed = (
        P(dp, mp, None, None),
        P(dp + mp, None, None, None),
        P(),
        P(),
        P(mp, None),
        P(mp, None),
        P(mp, None),
        P(dp + mp, None, None),
        P(dp + mp, None, None),
        P(dp + mp, None, None),
        P(dp + mp, None, None),
    )
    return jax.shard_map(
        local, mesh=wide, in_specs=placed, out_specs=(P(mp, None), P(mp, None)), check_vma=False
    )
```

```python
import functools

import jax
import jax.numpy as jnp
import numpy as np
from jax import lax
from jax.experimental import pallas as pl
from jax.experimental.pallas import tpu as pltpu
from jax.sharding import Mesh, PartitionSpec as P

NORM_EPS = 1e-05
CLIP_LOG = 2.0
KL_COEF = 0.25

X, ZL, C, Y, ZH = 4, 4, 2, 4, 4
WIDTH = 3072
TOKENS = 2048
RANK = 64
ROWS = 256
KY = WIDTH // Y
KM = KY // ZH
TM = TOKENS // (Y * ZH)
NB = TOKENS // (C * X)
PIECE = KY + ZH * 16
SHIFTS = (0, 1, 3, 2)
LANES = 384

bf16 = jnp.bfloat16
f32 = jnp.float32


def pairs(step):
    sizes = (X, C, Y)
    found = []
    for index in np.ndindex(*sizes):
        to = tuple(t % s for t, s in zip(step(*index), sizes))
        found.append(
            (int(np.ravel_multi_index(index, sizes)), int(np.ravel_multi_index(to, sizes)))
        )
    return found


def shift_first(v, k):
    return lax.ppermute(v, ("x", "c", "y"), pairs(lambda x, c, y: (x + k * (c == 0), c, y + k * (c == 1))))


def shift_second(v, k):
    return lax.ppermute(v, ("x", "c", "y"), pairs(lambda x, c, y: (x + k * (c == 1), c, y + k * (c == 0))))


def swap_cores(v):
    return lax.ppermute(v, "c", [(0, 1), (1, 0)])


def bdot(a, b, dims):
    return lax.dot_general(a, b, (dims, ((), ())), preferred_element_type=f32)


def normalize(hid, gain, normed, offset):
    step = 32

    def norm(i, carry):
        v = hid[pl.ds(pl.multiple_of(i * step, step), step), :].astype(f32)
        ms = jnp.sum(v * v, axis=-1, keepdims=True) * (1.0 / WIDTH)
        n = (v * lax.rsqrt(ms + NORM_EPS) * gain[...]).astype(bf16)
        normed[pl.ds(pl.multiple_of(offset + i * step, step), step), :] = n
        return carry

    lax.fori_loop(0, ROWS // step, norm, 0, unroll=2)


def policy_kernel(hid, gain, normed):
    normalize(hid, gain, normed, 0)


def fold(v):
    return v[:, 0:128] + v[:, 128:256]


def total_of(v):
    return jnp.sum(v, axis=-1, keepdims=True)


def kernel(
    place, pol_hbm, ref_hbm, ref_gain, rows8,
    p0, p1, p2, p3, p4, p5, p6, p7,
    keep, give,
    held, extra, normed, acc, up, down, low_t, grad, hid, sems, extra_sems,
):
    x, y, c = place[0], place[1], place[2]
    parts = (p0, p1, p2, p3, p4, p5, p6, p7)
    rows = pltpu.make_async_copy(ref_hbm, hid, sems.at[8])
    policy = pltpu.make_async_copy(pol_hbm, normed.at[pl.ds(0, ROWS)], sems.at[9])
    rows.start()
    policy.start()

    def place_of(i, q):
        core = c if i < 4 else 1 - c
        k1, k2 = SHIFTS[q], SHIFTS[i % 4]
        kx = jnp.where(core == 0, k1, k2)
        ky = jnp.where(core == 0, k2, k1)
        return core, lax.rem(x + X - kx, X), lax.rem(y + Y - ky, Y)

    def fetch(i, q):
        core, xq, ys = place_of(i, q)
        j = core * X + xq
        pltpu.make_async_copy(
            parts[i].at[q, pl.ds(0, KY)],
            held.at[j, pl.ds(pl.multiple_of(ys * KY, KY), KY)],
            sems.at[j],
        ).start()

    for half in range(2):
        for step in range(4):

            @pl.when(place_of(half * 4, 0)[0] == 0)
            def _(half=half, step=step):
                for n in range(4):
                    fetch(half * 4 + n, step)

            @pl.when(place_of(half * 4, 0)[0] == 1)
            def _(half=half, step=step):
                for n in range(4):
                    fetch(half * 4 + step, n)

    factors = [
        pltpu.make_async_copy(parts[i].at[:, pl.ds(KY, ZH * 16)], extra.at[i], extra_sems.at[i])
        for i in range(8)
    ]
    for copy in factors:
        copy.start()

    rows.wait()
    normalize(hid, ref_gain, normed, ROWS)

    policy.wait()

    def columns(s, carry):
        core = jnp.where(s < X, c, 1 - c)
        q = lax.rem(s, X)
        shift = jnp.where(q == 2, SHIFTS[2], jnp.where(q == 3, SHIFTS[3], q))
        j = core * X + lax.rem(x + X - shift, X)
        pltpu.make_async_copy(held.at[j], held.at[j], sems.at[j]).wait()
        for which in range(2):
            at = slice(which * ROWS, (which + 1) * ROWS)
            acc[j, at] = bdot(normed[at, :], held[j], ((1,), (0,)))
        return carry

    lax.fori_loop(0, C * X, columns, 0)

    for copy in factors:
        copy.wait()
    for i in range(8):

        @pl.when(place_of(i, 0)[0] == 0)
        def _(i=i):
            for q in range(4):
                _, xq, ys = place_of(i, q)
                at = pl.ds(pl.multiple_of(xq * 16, 16), 16)
                for z in range(ZH):
                    up[ys, at, z * TM : (z + 1) * TM] = extra[i, q, z * 16 : (z + 1) * 16, 0:TM]

        @pl.when(place_of(i, 0)[0] == 1)
        def _(i=i):
            for q in range(4):
                _, xq, ys = place_of(i, q)
                at = pl.ds(pl.multiple_of(xq * 16, 16), 16)
                down[ys, at, :] = jnp.concatenate(
                    [extra[i, q, z * 16 : (z + 1) * 16, 0:KM] for z in range(ZH)], axis=1
                )

    low = jnp.zeros((ROWS, RANK), f32)
    for k in range(Y):
        low += bdot(normed[0:ROWS, k * KY : (k + 1) * KY], down[k], ((1,), (1,)))
    low16 = low.astype(bf16)
    low_t[...] = low.T.astype(bf16)

    cols = rows8[...].T
    acts = cols[:, 0:1].astype(jnp.int32)
    mask, old, adv = cols[:, 1:2], cols[:, 2:3], cols[:, 3:4]
    iota = lax.broadcasted_iota(jnp.int32, (ROWS, NB), 1)

    def up_part(j):
        return up[j // 2, :, (j % 2) * NB : (j % 2 + 1) * NB]

    s_pol = jnp.zeros((ROWS, 128), f32)
    s_ref = jnp.zeros((ROWS, 128), f32)
    hit = jnp.zeros((ROWS, 128), f32)
    for j in range(8):
        v = acc[j, 0:ROWS] + bdot(low16, up_part(j), ((1,), (0,)))
        acc[j, 0:ROWS] = v
        s_pol += fold(jnp.exp(v))
        hit += fold(jnp.where(iota == acts - j * NB, v, 0.0))
        s_ref += fold(jnp.exp(acc[j, ROWS:]))
    lse_pol, lse_ref = jnp.log(total_of(s_pol)), jnp.log(total_of(s_ref))
    taken = total_of(hit) - lse_pol
    t = jnp.tanh((taken - old) / CLIP_LOG)
    pull = mask * (adv * jnp.exp(CLIP_LOG * t) * (1.0 - t * t))
    div = jnp.zeros((ROWS, 128), f32)
    for j in range(8):
        logp = acc[j, 0:ROWS] - lse_pol
        gap = logp - (acc[j, ROWS:] - lse_ref).astype(bf16).astype(f32)
        p = jnp.exp(logp)
        div += fold(p * gap)
        acc[j, 0:ROWS] = p
        acc[j, ROWS:] = gap
    scale = mask * KL_COEF
    base = pull - scale * total_of(div)
    low_slopes = jnp.zeros((ROWS, RANK), f32)
    for j in range(8):
        s = acc[j, 0:ROWS] * (scale * acc[j, ROWS:] + base) - jnp.where(iota == acts - j * NB, pull, 0.0)
        s16 = s.astype(bf16)
        grad[:, j * NB : (j + 1) * NB] = bdot(low_t[...], s16, ((1,), (0,)))
        low_slopes += bdot(s16, up_part(j), ((1,), (1,)))
    low_slopes_t = low_slopes.T.astype(bf16)
    for k in range(Y):
        grad[:, TOKENS + k * KY : TOKENS + (k + 1) * KY] = bdot(low_slopes_t, normed[0:ROWS, k * KY : (k + 1) * KY], ((1,), (0,)))

    blank = jnp.zeros((8, LANES - TM - KM), f32)
    for out, core in ((keep, c), (give, 1 - c)):
        for xx in range(X):
            at = pl.ds(pl.multiple_of((xx * C + core) * 8, 8), 8)
            for m in range(Y * ZH):
                sums = jnp.concatenate(
                    [
                        grad[at, m * TM : (m + 1) * TM],
                        grad[at, TOKENS + m * KM : TOKENS + (m + 1) * KM],
                        blank,
                    ],
                    axis=1,
                )
                out[xx, m] = sums.astype(out.dtype)


def local(ref_hidden, pol_hidden, ref_gain, pol_gain, head, down_w, up_w, actions, present, old, adv):
    x, y, c = lax.axis_index("x"), lax.axis_index("y"), lax.axis_index("c")
    piece = lax.dynamic_slice(head, (0, (c * X + x) * NB), (KM, NB))
    up_t = jnp.pad(up_w.T, ((0, 0), (0, NB - TM)))
    down_t = jnp.pad(down_w.T, ((0, 0), (0, NB - KM)))
    extra = lax.dynamic_slice(jnp.where(c == 0, up_t, down_t), (x * 16, 0), (16, NB))
    piece = jnp.concatenate([piece, extra], axis=0)
    along_z = lax.all_to_all(
        jnp.broadcast_to(piece[None], (ZH, KM + 16, NB)), "zh", 0, 0, tiled=True
    )
    mine = jnp.concatenate(
        [along_z[:, :KM].reshape(KY, NB), along_z[:, KM:].reshape(ZH * 16, NB)], axis=0
    )
    four = jnp.stack([mine] + [shift_first(mine, k) for k in SHIFTS[1:]])
    own = [four] + [shift_second(four, k) for k in SHIFTS[1:]]
    other = [swap_cores(v) for v in own]

    ref_hidden, guard, pol_hidden = lax.optimization_barrier(
        (ref_hidden, swap_cores(mine[:16, :NB]), pol_hidden)
    )
    ref_rows = lax.all_to_all(
        ref_hidden.reshape(Y * ZH, ROWS // (Y * ZH), WIDTH), ("y", "zh"), 0, 0, tiled=True
    ).reshape(ROWS, WIDTH)
    pol_rows = pol_hidden.reshape(ROWS, WIDTH)
    rows8 = jnp.stack(
        [v.reshape(ROWS).astype(f32) for v in (actions, present, old, adv)]
        + [jnp.zeros((ROWS,), f32)] * 3
        + [guard[0].astype(f32)]
    )
    place = jnp.stack([x, y, c]).astype(jnp.int32)

    vmem = pl.BlockSpec(memory_space=pltpu.VMEM)
    hbm = pl.BlockSpec(memory_space=pl.ANY)
    pol_normed = pl.pallas_call(
        policy_kernel,
        out_shape=jax.ShapeDtypeStruct((ROWS, WIDTH), bf16),
        in_specs=[vmem, vmem],
        out_specs=vmem,
        compiler_params=pltpu.CompilerParams(vmem_limit_bytes=16 * 1024 * 1024),
        cost_estimate=pl.CostEstimate(
            flops=4 * ROWS * WIDTH, bytes_accessed=4 * ROWS * WIDTH, transcendentals=ROWS
        ),
    )(pol_rows, pol_gain.reshape(1, WIDTH))
    out = jax.ShapeDtypeStruct((X, Y * ZH, 8, LANES), f32)
    keep, give = pl.pallas_call(
        kernel,
        out_shape=(out, jax.ShapeDtypeStruct(out.shape, bf16)),
        in_specs=[pl.BlockSpec(memory_space=pltpu.SMEM), hbm, hbm, vmem, vmem] + [hbm] * 8,
        out_specs=(vmem, vmem),
        scratch_shapes=[
            pltpu.VMEM((C * X, WIDTH, NB), bf16),
            pltpu.VMEM((8, 4, ZH * 16, NB), bf16),
            pltpu.VMEM((2 * ROWS, WIDTH), bf16),
            pltpu.VMEM((C * X, 2 * ROWS, NB), f32),
            pltpu.VMEM((Y, RANK, TOKENS // Y), bf16),
            pltpu.VMEM((Y, RANK, KY), bf16),
            pltpu.VMEM((RANK, ROWS), bf16),
            pltpu.VMEM((RANK, TOKENS + WIDTH), f32),
            pltpu.VMEM((ROWS, WIDTH), bf16),
            pltpu.SemaphoreType.DMA((10,)),
            pltpu.SemaphoreType.DMA((8,)),
        ],
        compiler_params=pltpu.CompilerParams(vmem_limit_bytes=36 * 1024 * 1024),
        cost_estimate=pl.CostEstimate(
            flops=4 * ROWS * WIDTH * TOKENS, bytes_accessed=18 << 20, transcendentals=3 * ROWS * TOKENS
        ),
    )(
        place, pol_normed, ref_rows, ref_gain.reshape(1, WIDTH), rows8, *own, *other,
    )

    part = (keep + swap_cores(give).astype(f32)).astype(bf16)
    part = lax.all_to_all(part.reshape(X * Y, ZH, 8, LANES), ("x", "y"), 0, 0, tiled=True)
    part = part.astype(f32).sum(0).astype(bf16)
    part = jnp.broadcast_to(part[None], (ZL, ZH, 8, LANES)).reshape(ZL * ZH, 8, LANES)
    part = lax.all_to_all(part, ("zl", "zh"), 0, 0, tiled=True).astype(f32).sum(0)
    whole = lax.all_to_all(
        jnp.broadcast_to(part[None], (X * C, 8, LANES)), ("x", "c"), 0, 0, tiled=True
    ).reshape(RANK, LANES)
    return whole[:, TM : TM + KM].T, whole[:, :TM].T


def solution(mesh):
    wide = Mesh(mesh.devices.reshape(X, ZL, C, Y, ZH), ("x", "zl", "c", "y", "zh"))
    dp, mp = ("x", "zl", "c"), ("y", "zh")
    placed = (
        P(dp, mp, None, None),
        P(dp + mp, None, None, None),
        P(),
        P(),
        P(mp, None),
        P(mp, None),
        P(mp, None),
        P(dp + mp, None, None),
        P(dp + mp, None, None),
        P(dp + mp, None, None),
        P(dp + mp, None, None),
    )
    return jax.shard_map(
        local, mesh=wide, in_specs=placed, out_specs=(P(mp, None), P(mp, None)), check_vma=False
    )
```

```python
import functools

import jax
import jax.numpy as jnp
import numpy as np
from jax import lax
from jax.experimental import pallas as pl
from jax.experimental.pallas import tpu as pltpu
from jax.sharding import Mesh, PartitionSpec as P

NORM_EPS = 1e-05
CLIP_LOG = 2.0
KL_COEF = 0.25

X, ZL, C, Y, ZH = 4, 4, 2, 4, 4
WIDTH = 3072
TOKENS = 2048
RANK = 64
ROWS = 256
KY = WIDTH // Y
KM = KY // ZH
TM = TOKENS // (Y * ZH)
NB = TOKENS // (C * X)
PIECE = KY + ZH * 16
SHIFTS = (0, 1, 3, 2)
LANES = 384

bf16 = jnp.bfloat16
f32 = jnp.float32


def pairs(step):
    sizes = (X, C, Y)
    found = []
    for index in np.ndindex(*sizes):
        to = tuple(t % s for t, s in zip(step(*index), sizes))
        found.append(
            (int(np.ravel_multi_index(index, sizes)), int(np.ravel_multi_index(to, sizes)))
        )
    return found


def shift_first(v, k):
    return lax.ppermute(v, ("x", "c", "y"), pairs(lambda x, c, y: (x + k * (c == 0), c, y + k * (c == 1))))


def shift_second(v, k):
    return lax.ppermute(v, ("x", "c", "y"), pairs(lambda x, c, y: (x + k * (c == 1), c, y + k * (c == 0))))


def swap_cores(v):
    return lax.ppermute(v, "c", [(0, 1), (1, 0)])


def bdot(a, b, dims):
    return lax.dot_general(a, b, (dims, ((), ())), preferred_element_type=f32)


def normalize(hid, gain, normed, offset):
    step = 32

    def norm(i, carry):
        v = hid[pl.ds(pl.multiple_of(i * step, step), step), :].astype(f32)
        ms = jnp.sum(v * v, axis=-1, keepdims=True) * (1.0 / WIDTH)
        n = (v * lax.rsqrt(ms + NORM_EPS) * gain[...]).astype(bf16)
        normed[pl.ds(pl.multiple_of(offset + i * step, step), step), :] = n
        return carry

    lax.fori_loop(0, ROWS // step, norm, 0, unroll=2)


def policy_kernel(hid, gain, normed):
    normalize(hid, gain, normed, 0)


def fold(v):
    return v[:, 0:128] + v[:, 128:256]


def total_of(v):
    return jnp.sum(v, axis=-1, keepdims=True)


def kernel(
    place, pol_hbm, ref_hbm, ref_gain, rows8,
    p0, p1, p2, p3, p4, p5, p6, p7,
    keep, give,
    held, extra, normed, acc, up, down, low_t, grad, hid, sems, extra_sems,
):
    x, y, c = place[0], place[1], place[2]
    parts = (p0, p1, p2, p3, p4, p5, p6, p7)
    rows = pltpu.make_async_copy(ref_hbm, hid, sems.at[8])
    policy = pltpu.make_async_copy(pol_hbm, normed.at[pl.ds(0, ROWS)], sems.at[9])
    rows.start()
    policy.start()

    def place_of(i, q):
        core = c if i < 4 else 1 - c
        k1, k2 = SHIFTS[q], SHIFTS[i % 4]
        kx = jnp.where(core == 0, k1, k2)
        ky = jnp.where(core == 0, k2, k1)
        return core, lax.rem(x + X - kx, X), lax.rem(y + Y - ky, Y)

    def fetch(i, q):
        core, xq, ys = place_of(i, q)
        j = core * X + xq
        pltpu.make_async_copy(
            parts[i].at[q, pl.ds(0, KY)],
            held.at[j, pl.ds(pl.multiple_of(ys * KY, KY), KY)],
            sems.at[j],
        ).start()

    factors = [
        pltpu.make_async_copy(parts[i].at[:, pl.ds(KY, ZH * 16)], extra.at[i], extra_sems.at[i])
        for i in range(8)
    ]
    for copy in factors:
        copy.start()

    for half in range(2):
        for step in range(4):

            @pl.when(place_of(half * 4, 0)[0] == 0)
            def _(half=half, step=step):
                for n in range(4):
                    fetch(half * 4 + n, step)

            @pl.when(place_of(half * 4, 0)[0] == 1)
            def _(half=half, step=step):
                for n in range(4):
                    fetch(half * 4 + step, n)

    for copy in factors:
        copy.wait()
    for i in range(8):

        @pl.when(place_of(i, 0)[0] == 0)
        def _(i=i):
            for q in range(4):
                _, xq, ys = place_of(i, q)
                at = pl.ds(pl.multiple_of(xq * 16, 16), 16)
                for z in range(ZH):
                    up[ys, at, z * TM : (z + 1) * TM] = extra[i, q, z * 16 : (z + 1) * 16, 0:TM]

        @pl.when(place_of(i, 0)[0] == 1)
        def _(i=i):
            for q in range(4):
                _, xq, ys = place_of(i, q)
                at = pl.ds(pl.multiple_of(xq * 16, 16), 16)
                down[ys, at, :] = jnp.concatenate(
                    [extra[i, q, z * 16 : (z + 1) * 16, 0:KM] for z in range(ZH)], axis=1
                )

    policy.wait()
    low = jnp.zeros((ROWS, RANK), f32)
    for k in range(Y):
        low += bdot(normed[0:ROWS, k * KY : (k + 1) * KY], down[k], ((1,), (1,)))
    low16 = low.astype(bf16)
    low_t[...] = low.T.astype(bf16)

    rows.wait()
    normalize(hid, ref_gain, normed, ROWS)

    def columns(s, carry):
        core = jnp.where(s < X, c, 1 - c)
        q = lax.rem(s, X)
        shift = jnp.where(q == 2, SHIFTS[2], jnp.where(q == 3, SHIFTS[3], q))
        j = core * X + lax.rem(x + X - shift, X)
        pltpu.make_async_copy(held.at[j], held.at[j], sems.at[j]).wait()
        acc[j] = bdot(normed[...], held[j], ((1,), (0,)))
        return carry

    lax.fori_loop(0, C * X, columns, 0)

    cols = rows8[...].T
    acts = cols[:, 0:1].astype(jnp.int32)
    mask, old, adv = cols[:, 1:2], cols[:, 2:3], cols[:, 3:4]
    iota = lax.broadcasted_iota(jnp.int32, (ROWS, NB), 1)

    def up_part(j):
        return up[j // 2, :, (j % 2) * NB : (j % 2 + 1) * NB]

    s_pol = jnp.zeros((ROWS, 128), f32)
    s_ref = jnp.zeros((ROWS, 128), f32)
    hit = jnp.zeros((ROWS, 128), f32)
    for j in range(8):
        v = acc[j, 0:ROWS] + bdot(low16, up_part(j), ((1,), (0,)))
        acc[j, 0:ROWS] = v
        s_pol += fold(jnp.exp(v))
        hit += fold(jnp.where(iota == acts - j * NB, v, 0.0))
        s_ref += fold(jnp.exp(acc[j, ROWS:]))
    lse_pol, lse_ref = jnp.log(total_of(s_pol)), jnp.log(total_of(s_ref))
    taken = total_of(hit) - lse_pol
    t = jnp.tanh((taken - old) / CLIP_LOG)
    pull = mask * (adv * jnp.exp(CLIP_LOG * t) * (1.0 - t * t))
    div = jnp.zeros((ROWS, 128), f32)
    for j in range(8):
        logp = acc[j, 0:ROWS] - lse_pol
        gap = logp - (acc[j, ROWS:] - lse_ref).astype(bf16).astype(f32)
        p = jnp.exp(logp)
        div += fold(p * gap)
        acc[j, 0:ROWS] = p
        acc[j, ROWS:] = gap
    scale = mask * KL_COEF
    base = pull - scale * total_of(div)
    low_slopes = jnp.zeros((ROWS, RANK), f32)
    for j in range(8):
        s = acc[j, 0:ROWS] * (scale * acc[j, ROWS:] + base) - jnp.where(iota == acts - j * NB, pull, 0.0)
        s16 = s.astype(bf16)
        grad[:, j * NB : (j + 1) * NB] = bdot(low_t[...], s16, ((1,), (0,)))
        low_slopes += bdot(s16, up_part(j), ((1,), (1,)))
    low_slopes_t = low_slopes.T.astype(bf16)
    for k in range(Y):
        grad[:, TOKENS + k * KY : TOKENS + (k + 1) * KY] = bdot(low_slopes_t, normed[0:ROWS, k * KY : (k + 1) * KY], ((1,), (0,)))

    blank = jnp.zeros((8, LANES - TM - KM), f32)
    for out, core in ((keep, c), (give, 1 - c)):
        for xx in range(X):
            at = pl.ds(pl.multiple_of((xx * C + core) * 8, 8), 8)
            for m in range(Y * ZH):
                sums = jnp.concatenate(
                    [
                        grad[at, m * TM : (m + 1) * TM],
                        grad[at, TOKENS + m * KM : TOKENS + (m + 1) * KM],
                        blank,
                    ],
                    axis=1,
                )
                out[xx, m] = sums.astype(out.dtype)


def local(ref_hidden, pol_hidden, ref_gain, pol_gain, head, down_w, up_w, actions, present, old, adv):
    x, y, c = lax.axis_index("x"), lax.axis_index("y"), lax.axis_index("c")
    piece = lax.dynamic_slice(head, (0, (c * X + x) * NB), (KM, NB))
    up_t = jnp.pad(up_w.T, ((0, 0), (0, NB - TM)))
    down_t = jnp.pad(down_w.T, ((0, 0), (0, NB - KM)))
    extra = lax.dynamic_slice(jnp.where(c == 0, up_t, down_t), (x * 16, 0), (16, NB))
    piece = jnp.concatenate([piece, extra], axis=0)
    along_z = lax.all_to_all(
        jnp.broadcast_to(piece[None], (ZH, KM + 16, NB)), "zh", 0, 0, tiled=True
    )
    mine = jnp.concatenate(
        [along_z[:, :KM].reshape(KY, NB), along_z[:, KM:].reshape(ZH * 16, NB)], axis=0
    )
    four = jnp.stack([mine] + [shift_first(mine, k) for k in SHIFTS[1:]])
    own = [four] + [shift_second(four, k) for k in SHIFTS[1:]]
    other = [swap_cores(v) for v in own]

    ref_hidden, guard, pol_hidden = lax.optimization_barrier(
        (ref_hidden, swap_cores(mine[:16, :NB]), pol_hidden)
    )
    ref_rows = lax.all_to_all(
        ref_hidden.reshape(Y * ZH, ROWS // (Y * ZH), WIDTH), ("y", "zh"), 0, 0, tiled=True
    ).reshape(ROWS, WIDTH)
    pol_rows = pol_hidden.reshape(ROWS, WIDTH)
    rows8 = jnp.stack(
        [v.reshape(ROWS).astype(f32) for v in (actions, present, old, adv)]
        + [jnp.zeros((ROWS,), f32)] * 3
        + [guard[0].astype(f32)]
    )
    place = jnp.stack([x, y, c]).astype(jnp.int32)

    vmem = pl.BlockSpec(memory_space=pltpu.VMEM)
    hbm = pl.BlockSpec(memory_space=pl.ANY)
    pol_normed = pl.pallas_call(
        policy_kernel,
        out_shape=jax.ShapeDtypeStruct((ROWS, WIDTH), bf16),
        in_specs=[vmem, vmem],
        out_specs=vmem,
        compiler_params=pltpu.CompilerParams(vmem_limit_bytes=16 * 1024 * 1024),
        cost_estimate=pl.CostEstimate(
            flops=4 * ROWS * WIDTH, bytes_accessed=4 * ROWS * WIDTH, transcendentals=ROWS
        ),
    )(pol_rows, pol_gain.reshape(1, WIDTH))
    out = jax.ShapeDtypeStruct((X, Y * ZH, 8, LANES), f32)
    keep, give = pl.pallas_call(
        kernel,
        out_shape=(out, jax.ShapeDtypeStruct(out.shape, bf16)),
        in_specs=[pl.BlockSpec(memory_space=pltpu.SMEM), hbm, hbm, vmem, vmem] + [hbm] * 8,
        out_specs=(vmem, vmem),
        scratch_shapes=[
            pltpu.VMEM((C * X, WIDTH, NB), bf16),
            pltpu.VMEM((8, 4, ZH * 16, NB), bf16),
            pltpu.VMEM((2 * ROWS, WIDTH), bf16),
            pltpu.VMEM((C * X, 2 * ROWS, NB), f32),
            pltpu.VMEM((Y, RANK, TOKENS // Y), bf16),
            pltpu.VMEM((Y, RANK, KY), bf16),
            pltpu.VMEM((RANK, ROWS), bf16),
            pltpu.VMEM((RANK, TOKENS + WIDTH), f32),
            pltpu.VMEM((ROWS, WIDTH), bf16),
            pltpu.SemaphoreType.DMA((10,)),
            pltpu.SemaphoreType.DMA((8,)),
        ],
        compiler_params=pltpu.CompilerParams(vmem_limit_bytes=36 * 1024 * 1024),
        cost_estimate=pl.CostEstimate(
            flops=4 * ROWS * WIDTH * TOKENS, bytes_accessed=18 << 20, transcendentals=3 * ROWS * TOKENS
        ),
    )(
        place, pol_normed, ref_rows, ref_gain.reshape(1, WIDTH), rows8, *own, *other,
    )

    part = (keep + swap_cores(give).astype(f32)).astype(bf16)
    part = lax.all_to_all(part.reshape(X * Y, ZH, 8, LANES), ("x", "y"), 0, 0, tiled=True)
    part = part.astype(f32).sum(0).astype(bf16)
    part = jnp.broadcast_to(part[None], (ZL, ZH, 8, LANES)).reshape(ZL * ZH, 8, LANES)
    part = lax.all_to_all(part, ("zl", "zh"), 0, 0, tiled=True).astype(f32).sum(0)
    whole = lax.all_to_all(
        jnp.broadcast_to(part[None], (X * C, 8, LANES)), ("x", "c"), 0, 0, tiled=True
    ).reshape(RANK, LANES)
    return whole[:, TM : TM + KM].T, whole[:, :TM].T


def solution(mesh):
    wide = Mesh(mesh.devices.reshape(X, ZL, C, Y, ZH), ("x", "zl", "c", "y", "zh"))
    dp, mp = ("x", "zl", "c"), ("y", "zh")
    placed = (
        P(dp, mp, None, None),
        P(dp + mp, None, None, None),
        P(),
        P(),
        P(mp, None),
        P(mp, None),
        P(mp, None),
        P(dp + mp, None, None),
        P(dp + mp, None, None),
        P(dp + mp, None, None),
        P(dp + mp, None, None),
    )
    return jax.shard_map(
        local, mesh=wide, in_specs=placed, out_specs=(P(mp, None), P(mp, None)), check_vma=False
    )
```
